1024 devices in a mesh: fsdp: 64 (over y_hi, z), mp: 16 (over y_lo, x, core).
Axes of the slice: x: 4, y: 4 (y_hi: 2, y_lo: 2; y = y_hi * 2 + y_lo), z: 32, core: 2. Of those that a mesh axis runs over, the one named last changes fastest.
Arguments:
- attn_out: bfloat16 [2048, 16384], P('mp', 'fsdp'), may hold values from -0.125 to 0.125
- grad_out: bfloat16 [2048, 16384], P('fsdp', 'mp'), may hold values from -6 to 6
- weight: bfloat16 [16384, 16384], P('fsdp', 'mp'), may hold values from -0.046875 to 0.046875
Outputs:
- grad_in: bfloat16 [2048, 16384], P('mp', 'fsdp')
- grad_weight: float32 [16384, 16384], P('fsdp', 'mp')
The draws below stay inside these ranges and needn't reach their ends.
All inputs are finite; a program needn't handle non-finite values.
Results may differ from the reference program's by a relative error of at most 0.001.
Values may be sent and summed in bfloat16 or wider, within the bound.
A program may use at most 32 MiB of HBM per device.

```python
import jax
import jax.numpy as jnp

HD = 16384
D = 16384
TOKENS = 2048


def steps_of(own_key, dims, cuts, least, high):
    loudness, own = 1.0, jax.random.fold_in(own_key, 6)
    for dim, blocks in cuts:
        heights = jnp.exp(jax.random.uniform(jax.random.fold_in(own, dim), (blocks,), jnp.float32, least / len(cuts), high / len(cuts)))
        loudness = loudness * jnp.repeat(heights, dims[dim] // blocks).reshape([-1 if axis == dim else 1 for axis in range(len(dims))])
    return loudness


def centred(stream_key, dims, scale, limit, shards=(), dtype=jnp.bfloat16):
    result = scale * jax.random.normal(stream_key, dims, jnp.float32)
    if shards:
        result = result * steps_of(stream_key, dims, shards, -0.22, 0.18)
    return jnp.clip(result, -limit, limit).astype(dtype)


def setup_inputs(seed: int = 0) -> dict:
    splits = jax.random.split(jax.random.key(seed), 4)
    return {
        "attn_out": centred(splits[0], (TOKENS, HD), (TOKENS ** -0.5), 0.125, ((0, 16), (1, 64))),
        "grad_out": centred(splits[1], (TOKENS, D), 1.0, 6.0, ((0, 64), (1, 16))),
        "weight": centred(splits[2], (HD, D), D ** -0.5, 0.046875, ((0, 64), (1, 16))),
    }


def reference(attn_out, grad_out, weight):
    grad_weight = jnp.dot(attn_out.T, grad_out, preferred_element_type=jnp.float32)
    grad_in = jnp.dot(grad_out, weight.T, preferred_element_type=jnp.float32).astype(jnp.bfloat16)
    return grad_in, grad_weight
```

```python
import functools

import jax
import jax.numpy as jnp
from jax import lax
from jax.experimental import pallas as pl
from jax.experimental.pallas import tpu as pltpu
from jax.sharding import PartitionSpec as P

MESH = pl.DeviceIdType.MESH
NZ = 32
NM = 16
TOK = 32
HALF = 16
FAR = NZ // 2


def kernel(
    attn_ref, grad_ref, w_ref, gin_ref, gw_ref,
    grads, feats, parts, landed, total,
    x_send, x_recv, r_send, r_recv, l_send, l_recv, a_send, a_recv, p_send, p_recv, o_sem,
):
    f, me = lax.axis_index("fsdp"), lax.axis_index("mp")
    z, yh = lax.rem(f, NZ), f // NZ
    right = yh * NZ + lax.rem(z + 1, NZ)
    left = yh * NZ + lax.rem(z + NZ - 1, NZ)
    partner = (1 - yh) * NZ + z

    barrier = pltpu.get_barrier_semaphore()
    for dev in (right, left, partner):
        pl.semaphore_signal(barrier, inc=1, device_id=(dev, me), device_id_type=MESH)
    for k in range(1, NM):
        pl.semaphore_signal(barrier, inc=1, device_id=(f, lax.rem(me + k, NM)), device_id_type=MESH)
    pl.semaphore_wait(barrier, 3 + NM - 1)

    def row(p, pos):
        half = lax.rem(yh + p, 2)
        return pl.multiple_of((half * NZ + pos) * TOK, TOK)

    def behind(s):
        return lax.rem(z - s + NZ, NZ)

    def ahead(s):
        return lax.rem(z + s, NZ)

    def ring(rightward, s, q):
        p, c = q // 2, q % 2
        pos = behind(s) if rightward else ahead(s)
        ref = grads.at[pl.ds(pl.multiple_of(row(p, pos) + c * HALF, HALF), HALF)]
        send, recv = (r_send, r_recv) if rightward else (l_send, l_recv)
        return pltpu.make_async_remote_copy(
            src_ref=ref, dst_ref=ref, send_sem=send.at[s, q], recv_sem=recv.at[s, q],
            device_id=(right if rightward else left, me), device_id_type=MESH,
        )

    def arrived(rightward, s, q):
        p, c = q // 2, q % 2
        pos = behind(s) if rightward else ahead(s)
        ref = grads.at[pl.ds(pl.multiple_of(row(p, pos) + c * HALF, HALF), HALF)]
        send, recv = (r_send, r_recv) if rightward else (l_send, l_recv)
        pltpu.make_async_remote_copy(
            src_ref=ref, dst_ref=ref, send_sem=send.at[s - 1, q], recv_sem=recv.at[s - 1, q],
            device_id=(right if rightward else left, me), device_id_type=MESH,
        ).wait_recv()

    def swap(c, p=0):
        ref = grads.at[pl.ds(pl.multiple_of(row(p, z) + c * HALF, HALF), HALF)]
        return pltpu.make_async_remote_copy(
            src_ref=ref, dst_ref=ref, send_sem=x_send.at[c], recv_sem=x_recv.at[c],
            device_id=(partner, me), device_id_type=MESH,
        )

    def feature(k):
        return pltpu.make_async_remote_copy(
            src_ref=attn_ref, dst_ref=feats.at[pl.ds(pl.multiple_of(me * 128, 128), 128)],
            send_sem=a_send.at[k], recv_sem=a_recv.at[k],
            device_id=(f, lax.rem(me + k, NM)), device_id_type=MESH,
        )

    def partial(p, pos):
        first = row(p, pos)
        owner = first // 128
        k = lax.rem(owner - me + NM, NM)
        j = lax.rem(pos, 4)
        return k, pltpu.make_async_remote_copy(
            src_ref=parts.at[pl.ds(first, TOK)],
            dst_ref=landed.at[k, pl.ds(pl.multiple_of(j * TOK, TOK), TOK)],
            send_sem=p_send.at[k, j], recv_sem=p_recv.at[k, j],
            device_id=(f, owner), device_id_type=MESH,
        )

    grads[pl.ds(row(0, z), TOK)] = grad_ref[...]
    for c in range(2):
        swap(c).start()
    for q in range(2):
        ring(True, 0, q).start()
        ring(False, 0, q).start()
    for k in range(1, NM):
        feature(k).start()
    feats[pl.ds(pl.multiple_of(me * 128, 128), 128)] = attn_ref[...]
    total[...] = jnp.zeros_like(total)
    for c in range(2):
        swap(c, 1).wait_recv()
        ring(True, 0, 2 + c).start()
        ring(False, 0, 2 + c).start()

    def both(s):
        return [(p, pos) for pos in (behind(s), ahead(s)) for p in (0, 1)]

    def rows_of(ref, pieces, cols=slice(None)):
        return jnp.concatenate([ref[pl.ds(row(p, pos), TOK), cols] for p, pos in pieces], axis=0)

    def input_part(pieces):
        out = lax.dot_general(
            rows_of(grads, pieces), w_ref[...], (((1,), (1,)), ((), ())),
            preferred_element_type=jnp.float32,
        )
        for i, (p, pos) in enumerate(pieces):
            parts[pl.ds(row(p, pos), TOK)] = out[i * TOK : (i + 1) * TOK]
        for p, pos in pieces:
            k, copy = partial(p, pos)

            @pl.when(k != 0)
            def _():
                copy.start()

    def weight_part(pieces, cols):
        total[:, cols] += lax.dot_general(
            rows_of(feats, pieces), rows_of(grads, pieces, cols), (((0,), (0,)), ((), ())),
            preferred_element_type=jnp.float32,
        )

    own = [(0, z), (1, z)]
    far = [(0, ahead(FAR)), (1, ahead(FAR))]
    low, high = slice(0, 512), slice(512, 1024)
    input_part(own)

    def forward(s, q, last_right, last_left):
        arrived(True, s, q)
        if not last_right:
            ring(True, s, q).start()
        arrived(False, s, q)
        if not last_left:
            ring(False, s, q).start()

    def early(s, _):
        for q in range(4):
            forward(s, q, False, False)
            if q == 1:
                @pl.when(s > 1)
                def _():
                    input_part(both(s - 1))
        return 0

    lax.fori_loop(1, 9, early, 0)

    for k in range(1, NM):
        feature(k).wait_recv()

    def late(s, _):
        done = both(2 * (s - 8) - 1) + both(2 * (s - 8))
        for q in range(4):
            arrived(True, s, q)
            ring(True, s, q).start()
            arrived(False, s, q)

            @pl.when(s < FAR - 1)
            def _():
                ring(False, s, q).start()

            if q == 0:
                input_part(both(s - 1))
            if q == 1:
                weight_part(done, low)
            if q == 2:
                weight_part(done, high)
        return 0

    lax.fori_loop(9, FAR, late, 0)
    input_part(both(FAR - 1))
    weight_part(both(FAR - 1) + own, low)
    weight_part(both(FAR - 1) + own, high)
    for q in range(4):
        arrived(True, FAR, q)
    input_part(far)
    weight_part(far, slice(0, 1024))
    out = pltpu.make_async_copy(total, gw_ref, o_sem)
    out.start()

    mine = pl.multiple_of(me * 128, 128)
    summed = parts[pl.ds(mine, 128)]
    for k in range(1, NM):
        for j in range(4):
            pltpu.make_async_remote_copy(
                src_ref=parts.at[pl.ds(0, TOK)], dst_ref=landed.at[k, pl.ds(j * TOK, TOK)],
                send_sem=p_send.at[k, j], recv_sem=p_recv.at[k, j],
                device_id=(f, lax.rem(me + k, NM)), device_id_type=MESH,
            ).wait()
        summed = summed + landed[k]
    gin_ref[...] = summed.astype(gin_ref.dtype)

    for c in range(2):
        swap(c).wait_send()
    for k in range(1, NM):
        feature(k).wait_send()

    def drain(s, _):
        for q in range(4):
            ring(True, s, q).wait_send()

            @pl.when(s < FAR - 1)
            def _():
                ring(False, s, q).wait_send()
        return 0

    lax.fori_loop(0, FAR, drain, 0)
    out.wait()


def local(attn_out, grad_out, weight):
    vmem = pl.BlockSpec(memory_space=pltpu.VMEM)
    return pl.pallas_call(
        kernel,
        out_shape=(
            jax.ShapeDtypeStruct((128, 256), jnp.bfloat16),
            jax.ShapeDtypeStruct((256, 1024), jnp.float32),
        ),
        in_specs=[vmem] * 3,
        out_specs=(vmem, pl.BlockSpec(memory_space=pl.ANY)),
        scratch_shapes=[
            pltpu.VMEM((2048, 1024), jnp.bfloat16),
            pltpu.VMEM((2048, 256), jnp.bfloat16),
            pltpu.VMEM((2048, 256), jnp.float32),
            pltpu.VMEM((NM, 128, 256), jnp.float32),
            pltpu.VMEM((256, 1024), jnp.float32),
            pltpu.SemaphoreType.DMA((2,)),
            pltpu.SemaphoreType.DMA((2,)),
            pltpu.SemaphoreType.DMA((FAR, 4)),
            pltpu.SemaphoreType.DMA((FAR, 4)),
            pltpu.SemaphoreType.DMA((FAR, 4)),
            pltpu.SemaphoreType.DMA((FAR, 4)),
            pltpu.SemaphoreType.DMA((NM,)),
            pltpu.SemaphoreType.DMA((NM,)),
            pltpu.SemaphoreType.DMA((NM, 4)),
            pltpu.SemaphoreType.DMA((NM, 4)),
            pltpu.SemaphoreType.DMA,
        ],
        compiler_params=pltpu.CompilerParams(
            collective_id=0, has_side_effects=True, vmem_limit_bytes=40 << 20
        ),
    )(attn_out, grad_out, weight)


def solution(mesh):
    return jax.shard_map(
        local,
        mesh=mesh,
        in_specs=(P("mp", "fsdp"), P("fsdp", "mp"), P("fsdp", "mp")),
        out_specs=(P("mp", "fsdp"), P("fsdp", "mp")),
        check_vma=False,
    )
```

```python
import functools

import jax
import jax.numpy as jnp
from jax import lax
from jax.experimental import pallas as pl
from jax.experimental.pallas import tpu as pltpu
from jax.sharding import PartitionSpec as P

MESH = pl.DeviceIdType.MESH
NZ = 32
NM = 16
CHIPS = NM // 2
TOK = 32
HALF = 16
FAR = NZ // 2


def kernel(
    attn_hbm, grad_hbm, w_hbm, gin_ref, gw_ref,
    grads, feats, w_ref, kept, given, taken, landed, total,
    i_sem, x_send, x_recv, r_send, r_recv, l_send, l_recv,
    a_send, a_recv, m_send, m_recv, e_send, e_recv, p_send, p_recv, o_sem,
):
    f, me = lax.axis_index("fsdp"), lax.axis_index("mp")
    z, yh = lax.rem(f, NZ), f // NZ
    chip, core = me // 2, lax.rem(me, 2)
    mate = chip * 2 + (1 - core)
    right = yh * NZ + lax.rem(z + 1, NZ)
    left = yh * NZ + lax.rem(z + NZ - 1, NZ)
    partner = (1 - yh) * NZ + z

    own_rows = pl.ds(pl.multiple_of(f * TOK, TOK), TOK)
    own_feats = pl.ds(pl.multiple_of(me * 128, 128), 128)
    fetch = [
        pltpu.make_async_copy(grad_hbm, grads.at[own_rows], i_sem.at[0]),
        pltpu.make_async_copy(attn_hbm, feats.at[own_feats], i_sem.at[1]),
        pltpu.make_async_copy(w_hbm, w_ref, i_sem.at[2]),
    ]
    for copy in fetch:
        copy.start()

    barrier = pltpu.get_barrier_semaphore()
    for dev in (right, left, partner):
        pl.semaphore_signal(barrier, inc=1, device_id=(dev, me), device_id_type=MESH)
    for k in range(1, NM):
        pl.semaphore_signal(barrier, inc=1, device_id=(f, lax.rem(me + k, NM)), device_id_type=MESH)
    pl.semaphore_wait(barrier, 3 + NM - 1)

    def token(half, pos):
        return pl.multiple_of((half * NZ + pos) * TOK, TOK)

    def row(p, pos):
        return token(lax.rem(yh + p, 2), pos)

    def behind(s):
        return lax.rem(z - s + NZ, NZ)

    def ahead(s):
        return lax.rem(z + s, NZ)

    def hop(rightward, at, s, q):
        p, c = q // 2, q % 2
        pos = behind(at) if rightward else ahead(at)
        ref = grads.at[pl.ds(pl.multiple_of(row(p, pos) + c * HALF, HALF), HALF)]
        send, recv = (r_send, r_recv) if rightward else (l_send, l_recv)
        return pltpu.make_async_remote_copy(
            src_ref=ref, dst_ref=ref, send_sem=send.at[s, q], recv_sem=recv.at[s, q],
            device_id=(right if rightward else left, me), device_id_type=MESH,
        )

    def ring(rightward, s, q):
        return hop(rightward, s, s, q)

    def arrived(rightward, s, q):
        hop(rightward, s, s - 1, q).wait_recv()

    def swap(c, p=0):
        ref = grads.at[pl.ds(pl.multiple_of(row(p, z) + c * HALF, HALF), HALF)]
        return pltpu.make_async_remote_copy(
            src_ref=ref, dst_ref=ref, send_sem=x_send.at[c], recv_sem=x_recv.at[c],
            device_id=(partner, me), device_id_type=MESH,
        )

    def feature(k, incoming=False):
        src = lax.rem(chip - k + CHIPS, CHIPS) * 2 + core if incoming else me
        ref = feats.at[pl.ds(pl.multiple_of(src * 128, 128), 128)]
        return pltpu.make_async_remote_copy(
            src_ref=ref, dst_ref=ref, send_sem=a_send.at[k], recv_sem=a_recv.at[k],
            device_id=(f, lax.rem(chip + k, CHIPS) * 2 + core), device_id_type=MESH,
        )

    def pass_on(k, incoming=False):
        src = lax.rem(chip - k + CHIPS, CHIPS) * 2 + (1 - core if incoming else core)
        ref = feats.at[pl.ds(pl.multiple_of(src * 128, 128), 128)]
        return pltpu.make_async_remote_copy(
            src_ref=ref, dst_ref=ref, send_sem=m_send.at[k], recv_sem=m_recv.at[k],
            device_id=(f, mate), device_id_type=MESH,
        )

    def exchange(s, rows):
        return pltpu.make_async_remote_copy(
            src_ref=given.at[s, pl.ds(0, rows)], dst_ref=taken.at[s, pl.ds(0, rows)],
            send_sem=e_send.at[s], recv_sem=e_recv.at[s],
            device_id=(f, mate), device_id_type=MESH,
        )

    def deliver(s, i, pos):
        owner = core * CHIPS + pos // 4
        j = lax.rem(pos, 4)
        return owner, pltpu.make_async_remote_copy(
            src_ref=kept.at[s, pl.ds(i * TOK, TOK)],
            dst_ref=landed.at[chip, pl.ds(pl.multiple_of(j * TOK, TOK), TOK)],
            send_sem=p_send.at[pos], recv_sem=p_recv.at[chip, j],
            device_id=(f, owner), device_id_type=MESH,
        )

    fetch[0].wait()
    for q in range(2):
        ring(True, 0, q).start()
        ring(False, 0, q).start()
    for c in range(2):
        swap(c).start()
    fetch[1].wait()
    fetch[2].wait()
    pass_on(0).start()
    total[...] = jnp.zeros_like(total)
    for c in range(2):
        swap(c, 1).wait_recv()
        ring(True, 0, 2 + c).start()
        ring(False, 0, 2 + c).start()

    def both(s):
        return [(p, pos) for pos in (behind(s), ahead(s)) for p in (0, 1)]

    def input_part(s, places):
        n = len(places) * TOK
        lhs = [grads[pl.ds(token(half, pos), TOK), :] for half in (core, 1 - core) for pos in places]
        out = lax.dot_general(
            jnp.concatenate(lhs, axis=0), w_ref[...], (((1,), (1,)), ((), ())),
            preferred_element_type=jnp.float32,
        )
        given[s, pl.ds(0, n)] = out[n:]
        exchange(s, n).start()
        kept[s, pl.ds(0, n)] = out[:n]

    def combine(s, places):
        n = len(places) * TOK
        exchange(s, n).wait_recv()
        kept[s, pl.ds(0, n)] += taken[s, pl.ds(0, n)]
        for i, pos in enumerate(places):
            owner, copy = deliver(s, i, pos)

            @pl.when(owner != me)
            def _():
                copy.start()

            @pl.when(owner == me)
            def _():
                landed[chip, pl.ds(pl.multiple_of(lax.rem(pos, 4) * TOK, TOK), TOK)] = kept[s, pl.ds(i * TOK, TOK)]

    def rows_of(ref, pieces, cols=slice(None)):
        return jnp.concatenate([ref[pl.ds(row(p, pos), TOK), cols] for p, pos in pieces], axis=0)

    def weight_part(pieces, cols):
        total[:, cols] += lax.dot_general(
            rows_of(feats, pieces), rows_of(grads, pieces, cols), (((0,), (0,)), ((), ())),
            preferred_element_type=jnp.float32,
        )

    def pair(s):
        return [behind(s), ahead(s)]

    own = [(0, z), (1, z)]
    far = [(0, ahead(FAR)), (1, ahead(FAR))]
    low, high = slice(0, 512), slice(512, 1024)
    input_part(0, [z])

    def early(s, _):
        for q in range(4):
            arrived(True, s, q)
            ring(True, s, q).start()
            arrived(False, s, q)
            ring(False, s, q).start()
            if q == 0:
                @pl.when(s > 2)
                def _():
                    combine(s - 2, pair(s - 2))

                @pl.when(s > 1)
                def _():
                    input_part(s - 1, pair(s - 1))
            if q % 2 == 1:
                k = 2 * (s - 1) + (q + 1) // 2

                @pl.when(k < CHIPS)
                def _():
                    feature(k).start()

                back = k - CHIPS

                @pl.when((back > 0) & (back < CHIPS))
                def _():
                    feature(back, True).wait_recv()
                    pass_on(back).start()
        return 0

    lax.fori_loop(1, 9, early, 0)

    combine(0, [z])
    for k in range(CHIPS):
        pass_on(k, True).wait_recv()

    def late(s, _):
        done = both(2 * (s - 8) - 1) + both(2 * (s - 8))
        for q in range(4):
            arrived(True, s, q)
            ring(True, s, q).start()
            arrived(False, s, q)

            @pl.when(s < FAR - 1)
            def _():
                ring(False, s, q).start()

            if q == 0:
                combine(s - 2, pair(s - 2))
                input_part(s - 1, pair(s - 1))
            if q == 1:
                weight_part(done, low)
            if q == 2:
                weight_part(done, high)
        return 0

    lax.fori_loop(9, FAR, late, 0)
    combine(FAR - 2, pair(FAR - 2))
    input_part(FAR - 1, pair(FAR - 1))
    weight_part(both(FAR - 1) + own, low)
    combine(FAR - 1, pair(FAR - 1))
    weight_part(both(FAR - 1) + own, high)
    for q in range(4):
        arrived(True, FAR, q)
    input_part(FAR, [ahead(FAR)])
    weight_part(far, slice(0, 1024))
    combine(FAR, [ahead(FAR)])
    out = pltpu.make_async_copy(total, gw_ref, o_sem)
    out.start()

    for c in range(CHIPS):
        for j in range(4):
            @pl.when((chip != c) | (core != me // CHIPS))
            def _():
                ref = landed.at[c, pl.ds(j * TOK, TOK)]
                pltpu.make_async_remote_copy(
                    src_ref=ref, dst_ref=ref, send_sem=p_send.at[0], recv_sem=p_recv.at[c, j],
                    device_id=(f, mate), device_id_type=MESH,
                ).wait_recv()
    summed = landed[0]
    for c in range(1, CHIPS):
        summed = summed + landed[c]
    gin_ref[...] = summed.astype(gin_ref.dtype)

    def sent(s, i, pos):
        owner, copy = deliver(s, i, pos)

        @pl.when(owner != me)
        def _():
            copy.wait_send()

    for c in range(2):
        swap(c).wait_send()
    pass_on(0).wait_send()
    for k in range(1, CHIPS):
        feature(k).wait_send()
        pass_on(k).wait_send()
    exchange(0, TOK).wait_send()
    exchange(FAR, TOK).wait_send()
    sent(0, 0, z)
    sent(FAR, 0, ahead(FAR))

    def drain(s, _):
        @pl.when(s > 0)
        def _():
            exchange(s, 2 * TOK).wait_send()
            for i, pos in enumerate(pair(s)):
                sent(s, i, pos)

        for q in range(4):
            ring(True, s, q).wait_send()

            @pl.when(s < FAR - 1)
            def _():
                ring(False, s, q).wait_send()
        return 0

    lax.fori_loop(0, FAR, drain, 0)
    out.wait()


def local(attn_out, grad_out, weight):
    vmem = pl.BlockSpec(memory_space=pltpu.VMEM)
    dma = pltpu.SemaphoreType.DMA
    args = [pltpu.with_memory_space_constraint(x, pltpu.HBM) for x in (attn_out, grad_out, weight)]
    return pl.pallas_call(
        kernel,
        out_shape=(
            jax.ShapeDtypeStruct((128, 256), jnp.bfloat16),
            jax.ShapeDtypeStruct((256, 1024), jnp.float32),
        ),
        in_specs=[pl.BlockSpec(memory_space=pltpu.HBM)] * 3,
        out_specs=(vmem, pl.BlockSpec(memory_space=pl.ANY)),
        scratch_shapes=[
            pltpu.VMEM((2048, 1024), jnp.bfloat16),
            pltpu.VMEM((2048, 256), jnp.bfloat16),
            pltpu.VMEM((256, 1024), jnp.bfloat16),
            pltpu.VMEM((FAR + 1, 2 * TOK, 256), jnp.float32),
            pltpu.VMEM((FAR + 1, 2 * TOK, 256), jnp.float32),
            pltpu.VMEM((FAR + 1, 2 * TOK, 256), jnp.float32),
            pltpu.VMEM((CHIPS, 128, 256), jnp.float32),
            pltpu.VMEM((256, 1024), jnp.float32),
            dma((3,)),
            dma((2,)),
            dma((2,)),
            dma((FAR, 4)),
            dma((FAR, 4)),
            dma((FAR, 4)),
            dma((FAR, 4)),
            dma((CHIPS,)),
            dma((CHIPS,)),
            dma((CHIPS,)),
            dma((CHIPS,)),
            dma((FAR + 1,)),
            dma((FAR + 1,)),
            dma((NZ,)),
            dma((CHIPS, 4)),
            dma,
        ],
        compiler_params=pltpu.CompilerParams(
            collective_id=0, has_side_effects=True, vmem_limit_bytes=40 << 20
        ),
    )(*args)


def solution(mesh):
    return jax.shard_map(
        local,
        mesh=mesh,
        in_specs=(P("mp", "fsdp"), P("fsdp", "mp"), P("fsdp", "mp")),
        out_specs=(P("mp", "fsdp"), P("fsdp", "mp")),
        check_vma=False,
    )
```

```python
import functools

import jax
import jax.numpy as jnp
from jax import lax
from jax.experimental import pallas as pl
from jax.experimental.pallas import tpu as pltpu
from jax.sharding import PartitionSpec as P

MESH = pl.DeviceIdType.MESH
NZ = 32
NM = 16
CHIPS = NM // 2
TOK = 32
HALF = 16
FAR = NZ // 2


def kernel(
    attn_hbm, grad_hbm, w_hbm, gin_ref, total,
    grads, feats, w_ref, kept, given, taken, landed,
    i_sem, x_send, x_recv, d_send, d_recv, t_send, t_recv,
    a_send, a_recv, m_send, m_recv, e_send, e_recv, p_send, p_recv,
):
    f, me = lax.axis_index("fsdp"), lax.axis_index("mp")
    z, yh = lax.rem(f, NZ), f // NZ
    chip, core = me // 2, lax.rem(me, 2)
    mate = chip * 2 + (1 - core)
    down = yh * NZ + lax.rem(z + NZ - 1, NZ)
    up = yh * NZ + lax.rem(z + 1, NZ)
    partner = (1 - yh) * NZ + z

    own_rows = pl.ds(pl.multiple_of(f * TOK, TOK), TOK)
    own_feats = pl.ds(pl.multiple_of(me * 128, 128), 128)
    fetch = [
        pltpu.make_async_copy(grad_hbm, grads.at[own_rows], i_sem.at[0]),
        pltpu.make_async_copy(attn_hbm, feats.at[own_feats], i_sem.at[1]),
        pltpu.make_async_copy(w_hbm, w_ref, i_sem.at[2]),
    ]
    for copy in fetch:
        copy.start()

    barrier = pltpu.get_barrier_semaphore()
    for dev in (down, up, partner):
        pl.semaphore_signal(barrier, inc=1, device_id=(dev, me), device_id_type=MESH)
    for k in range(1, NM):
        pl.semaphore_signal(barrier, inc=1, device_id=(f, lax.rem(me + k, NM)), device_id_type=MESH)
    pl.semaphore_wait(barrier, 3 + NM - 1)

    def token(half, pos):
        return pl.multiple_of((half * NZ + pos) * TOK, TOK)

    def row(p, pos):
        return token(lax.rem(yh + p, 2), pos)

    def above(s):
        return lax.rem(z + s, NZ)

    def below(s):
        return lax.rem(z - s + NZ, NZ)

    def hop(downward, at, s, q):
        p, c = q // 2, q % 2
        pos = above(at) if downward else below(at)
        ref = grads.at[pl.ds(pl.multiple_of(row(p, pos) + c * HALF, HALF), HALF)]
        send, recv = (d_send, d_recv) if downward else (t_send, t_recv)
        return pltpu.make_async_remote_copy(
            src_ref=ref, dst_ref=ref, send_sem=send.at[s, q], recv_sem=recv.at[s, q],
            device_id=(down if downward else up, me), device_id_type=MESH,
        )

    def ring(downward, s, q):
        return hop(downward, s, s, q)

    def arrived(downward, s, q):
        hop(downward, s, s - 1, q).wait_recv()

    def swap(c, p=0):
        ref = grads.at[pl.ds(pl.multiple_of(row(p, z) + c * HALF, HALF), HALF)]
        return pltpu.make_async_remote_copy(
            src_ref=ref, dst_ref=ref, send_sem=x_send.at[c], recv_sem=x_recv.at[c],
            device_id=(partner, me), device_id_type=MESH,
        )

    def feature(k, incoming=False):
        src = lax.rem(chip - k + CHIPS, CHIPS) * 2 + core if incoming else me
        ref = feats.at[pl.ds(pl.multiple_of(src * 128, 128), 128)]
        return pltpu.make_async_remote_copy(
            src_ref=ref, dst_ref=ref, send_sem=a_send.at[k], recv_sem=a_recv.at[k],
            device_id=(f, lax.rem(chip + k, CHIPS) * 2 + core), device_id_type=MESH,
        )

    def pass_on(k, incoming=False):
        src = lax.rem(chip - k + CHIPS, CHIPS) * 2 + (1 - core if incoming else core)
        ref = feats.at[pl.ds(pl.multiple_of(src * 128, 128), 128)]
        return pltpu.make_async_remote_copy(
            src_ref=ref, dst_ref=ref, send_sem=m_send.at[k], recv_sem=m_recv.at[k],
            device_id=(f, mate), device_id_type=MESH,
        )

    def exchange(s, rows):
        return pltpu.make_async_remote_copy(
            src_ref=given.at[s, pl.ds(0, rows)], dst_ref=taken.at[s, pl.ds(0, rows)],
            send_sem=e_send.at[s], recv_sem=e_recv.at[s],
            device_id=(f, mate), device_id_type=MESH,
        )

    def deliver(s, i, pos):
        owner = core * CHIPS + pos // 4
        j = lax.rem(pos, 4)
        return owner, pltpu.make_async_remote_copy(
            src_ref=kept.at[s, pl.ds(i * TOK, TOK)],
            dst_ref=landed.at[chip, pl.ds(pl.multiple_of(j * TOK, TOK), TOK)],
            send_sem=p_send.at[pos], recv_sem=p_recv.at[chip, j],
            device_id=(f, owner), device_id_type=MESH,
        )

    fetch[0].wait()
    for q in range(2):
        ring(True, 0, q).start()
        ring(False, 0, q).start()
    for c in range(2):
        swap(c).start()
    fetch[1].wait()
    fetch[2].wait()
    pass_on(0).start()
    total[...] = jnp.zeros_like(total)
    for c in range(2):
        swap(c, 1).wait_recv()
        ring(True, 0, 2 + c).start()
        ring(False, 0, 2 + c).start()

    def both(s):
        return [(p, pos) for pos in (above(s), below(s)) for p in (0, 1)]

    def input_part(s, places):
        n = len(places) * TOK
        lhs = [grads[pl.ds(token(half, pos), TOK), :] for half in (core, 1 - core) for pos in places]
        out = lax.dot_general(
            jnp.concatenate(lhs, axis=0), w_ref[...], (((1,), (1,)), ((), ())),
            preferred_element_type=jnp.float32,
        )
        given[s, pl.ds(0, n)] = out[n:]
        exchange(s, n).start()
        kept[s, pl.ds(0, n)] = out[:n]

    def combine(s, places):
        n = len(places) * TOK
        exchange(s, n).wait_recv()
        kept[s, pl.ds(0, n)] += taken[s, pl.ds(0, n)]
        for i, pos in enumerate(places):
            owner, copy = deliver(s, i, pos)

            @pl.when(owner != me)
            def _():
                copy.start()

            @pl.when(owner == me)
            def _():
                landed[chip, pl.ds(pl.multiple_of(lax.rem(pos, 4) * TOK, TOK), TOK)] = kept[s, pl.ds(i * TOK, TOK)]

    def rows_of(ref, pieces, cols=slice(None)):
        return jnp.concatenate([ref[pl.ds(row(p, pos), TOK), cols] for p, pos in pieces], axis=0)

    def weight_part(pieces, cols):
        total[:, cols] += lax.dot_general(
            rows_of(feats, pieces), rows_of(grads, pieces, cols), (((0,), (0,)), ((), ())),
            preferred_element_type=jnp.float32,
        )

    def pair(s):
        return [above(s), below(s)]

    own = [(0, z), (1, z)]
    far = [(0, below(FAR)), (1, below(FAR))]
    low, high = slice(0, 512), slice(512, 1024)
    input_part(0, [z])

    def early(s, _):
        for q in range(4):
            arrived(True, s, q)
            ring(True, s, q).start()
            arrived(False, s, q)
            ring(False, s, q).start()
            if q == 0:
                @pl.when(s > 2)
                def _():
                    combine(s - 2, pair(s - 2))

                @pl.when(s > 1)
                def _():
                    input_part(s - 1, pair(s - 1))
            if q % 2 == 1:
                k = 2 * (s - 1) + (q + 1) // 2

                @pl.when(k < CHIPS)
                def _():
                    feature(k).start()

                back = k - CHIPS

                @pl.when((back > 0) & (back < CHIPS))
                def _():
                    feature(back, True).wait_recv()
                    pass_on(back).start()
        return 0

    lax.fori_loop(1, 9, early, 0)

    combine(0, [z])
    for k in range(CHIPS):
        pass_on(k, True).wait_recv()

    def late(s, _):
        done = both(2 * (s - 8) - 1) + both(2 * (s - 8))
        for q in range(4):
            arrived(True, s, q)
            ring(True, s, q).start()
            arrived(False, s, q)

            @pl.when(s < FAR - 1)
            def _():
                ring(False, s, q).start()

            if q == 0:
                combine(s - 2, pair(s - 2))
                input_part(s - 1, pair(s - 1))
            if q == 1:
                weight_part(done, low)
            if q == 2:
                weight_part(done, high)
        return 0

    lax.fori_loop(9, FAR, late, 0)
    combine(FAR - 2, pair(FAR - 2))
    input_part(FAR - 1, pair(FAR - 1))
    weight_part(both(FAR - 1) + own, low)
    combine(FAR - 1, pair(FAR - 1))
    weight_part(both(FAR - 1) + own, high)
    for q in range(4):
        arrived(True, FAR, q)
    input_part(FAR, [below(FAR)])
    weight_part(far, slice(0, 1024))
    combine(FAR, [below(FAR)])

    def sent(s, i, pos):
        owner, copy = deliver(s, i, pos)

        @pl.when(owner != me)
        def _():
            copy.wait_send()

    for c in range(2):
        swap(c).wait_send()
    pass_on(0).wait_send()
    for k in range(1, CHIPS):
        feature(k).wait_send()
        pass_on(k).wait_send()
    exchange(0, TOK).wait_send()
    sent(0, 0, z)

    def drain(s, _):
        @pl.when((s > 0) & (s < FAR - 1))
        def _():
            exchange(s, 2 * TOK).wait_send()
            for i, pos in enumerate(pair(s)):
                sent(s, i, pos)

        for q in range(4):
            ring(True, s, q).wait_send()

            @pl.when(s < FAR - 1)
            def _():
                ring(False, s, q).wait_send()
        return 0

    lax.fori_loop(0, FAR, drain, 0)
    for c in range(CHIPS):
        for j in range(4):
            @pl.when((chip != c) | (core != me // CHIPS))
            def _():
                ref = landed.at[c, pl.ds(j * TOK, TOK)]
                pltpu.make_async_remote_copy(
                    src_ref=ref, dst_ref=ref, send_sem=p_send.at[0], recv_sem=p_recv.at[c, j],
                    device_id=(f, mate), device_id_type=MESH,
                ).wait_recv()
    summed = landed[0]
    for c in range(1, CHIPS):
        summed = summed + landed[c]
    gin_ref[...] = summed.astype(gin_ref.dtype)

    exchange(FAR - 1, 2 * TOK).wait_send()
    exchange(FAR, TOK).wait_send()
    for i, pos in enumerate(pair(FAR - 1)):
        sent(FAR - 1, i, pos)
    sent(FAR, 0, below(FAR))


def local(attn_out, grad_out, weight):
    vmem = pl.BlockSpec(memory_space=pltpu.VMEM)
    dma = pltpu.SemaphoreType.DMA
    args = [pltpu.with_memory_space_constraint(x, pltpu.HBM) for x in (attn_out, grad_out, weight)]
    return pl.pallas_call(
        kernel,
        out_shape=(
            jax.ShapeDtypeStruct((128, 256), jnp.bfloat16),
            jax.ShapeDtypeStruct((256, 1024), jnp.float32),
        ),
        in_specs=[pl.BlockSpec(memory_space=pltpu.HBM)] * 3,
        out_specs=(vmem, vmem),
        scratch_shapes=[
            pltpu.VMEM((2048, 1024), jnp.bfloat16),
            pltpu.VMEM((2048, 256), jnp.bfloat16),
            pltpu.VMEM((256, 1024), jnp.bfloat16),
            pltpu.VMEM((FAR + 1, 2 * TOK, 256), jnp.float32),
            pltpu.VMEM((FAR + 1, 2 * TOK, 256), jnp.float32),
            pltpu.VMEM((FAR + 1, 2 * TOK, 256), jnp.float32),
            pltpu.VMEM((CHIPS, 128, 256), jnp.float32),
            dma((3,)),
            dma((2,)),
            dma((2,)),
            dma((FAR, 4)),
            dma((FAR, 4)),
            dma((FAR, 4)),
            dma((FAR, 4)),
            dma((CHIPS,)),
            dma((CHIPS,)),
            dma((CHIPS,)),
            dma((CHIPS,)),
            dma((FAR + 1,)),
            dma((FAR + 1,)),
            dma((NZ,)),
            dma((CHIPS, 4)),
        ],
        compiler_params=pltpu.CompilerParams(
            collective_id=0, has_side_effects=True, vmem_limit_bytes=40 << 20
        ),
    )(*args)


def solution(mesh):
    return jax.shard_map(
        local,
        mesh=mesh,
        in_specs=(P("mp", "fsdp"), P("fsdp", "mp"), P("fsdp", "mp")),
        out_specs=(P("mp", "fsdp"), P("fsdp", "mp")),
        check_vma=False,
    )
```
